32 devices in a mesh: grp: 2 (over x), lon: 16 (over z, y, core).
Axes of the slice: x: 2, y: 2, z: 4, core: 2. Of those that a mesh axis runs over, the one named last changes fastest.
Arguments:
- fields: bfloat16 [64, 1536, 256], P('grp', 'lon'), parts along dimension 0, may hold values from -6 to 6
- zonal_coef: bfloat16 [32, 1536], replicated, may hold values from -0.15625 to 0.15625
- vert_taps: bfloat16 [15], replicated, may hold values from 0.019897461 to 0.14941406
Outputs:
- filtered: bfloat16 [64, 1536, 256], P('grp', 'lon'), parts along dimension 0
The draws below stay inside these ranges and needn't reach their ends.
There are 2 independent parts, one for each index of `grp`. The reference program is written for one: setup_inputs(seed, part) draws one part's arguments, and reference() takes and returns one part's arrays. A program takes and returns all parts, laid end to end along the dimension named above; an argument that names none is the same for every part. Nothing has to cross between parts.
All inputs are finite; a program needn't handle non-finite values.
Results may differ from the reference program's by a relative error of at most 0.0049.
Values may be sent and summed in bfloat16 or wider, within the bound.
No kernel may reach another device: no remote copies, remote signals or barrier semaphores. Data moves between devices by JAX's collectives and lax.ppermute only.
A program may use at most 128 MiB of HBM per device.

```python
import jax
import jax.numpy as jnp
from jax import lax

NLON = 1536
LAT = 32
FIELDS = 4
LEV = 64
TAPS = 15
COLS = 256


def level_of(stream_key, extent, split, low, high):
    def one(position, parts):
        draws = jax.random.uniform(jax.random.fold_in(jax.random.fold_in(stream_key, 6), position), (parts,), jnp.float32, low / len(split), high / len(split))
        return jnp.repeat(jnp.exp(draws), extent[position] // parts).reshape((-1,) + (1,) * (len(extent) - position - 1))

    level = one(*split[0])
    for cut in split[1:]:
        level = level * one(*cut)
    return level


def noise(stream_key, extent, width, most, split=(), kind=jnp.bfloat16):
    values = width * jax.random.normal(stream_key, extent, jnp.float32)
    if split:
        values = values * level_of(stream_key, extent, split, -0.22, 0.18)
    return jnp.clip(values, -most, most).astype(kind)


def setup_inputs(seed: int = 0, part: int = 0) -> dict:
    streams_of = jax.random.split(jax.random.key(seed), 4)
    part_splits = jax.random.split(jax.random.fold_in(streams_of[3], part), 4)
    fields = noise(part_splits[0], (LAT, NLON, COLS), 1.0, 6.0, ((1, 16),))
    zonal_coef = noise(streams_of[1], (LAT, NLON), NLON ** -0.5, 0.15625)
    vert_taps = jnp.clip(jax.random.uniform(streams_of[2], (TAPS,), jnp.float32, 0.019897461, 0.14941406), 0.019897461, 0.14941406).astype(jnp.bfloat16)
    return dict(fields=fields, zonal_coef=zonal_coef, vert_taps=vert_taps)


def band_matrix(vert_taps):
    half = (TAPS - 1) // 2
    upper = jnp.arange(LEV, dtype=jnp.int32)[:, None]
    lower = jnp.arange(LEV, dtype=jnp.int32)[None, :]
    offset = upper - lower
    index = jnp.clip(offset + half, 0, TAPS - 1).astype(jnp.int32)
    values = jnp.take(vert_taps, index)
    return jnp.where(jnp.abs(offset) <= half, values, jnp.zeros_like(values))


def reference(fields, zonal_coef, vert_taps):
    rows = jnp.arange(NLON, dtype=jnp.int32)
    index = ((rows[:, None] - rows[None, :]) % NLON).astype(jnp.int32)

    def one_lat(pair):
        coef_row, block = pair
        circ = jnp.take(coef_row, index)
        return jnp.dot(circ, block, preferred_element_type=jnp.float32).astype(jnp.bfloat16)

    zonal = lax.map(one_lat, (zonal_coef, fields))
    band = band_matrix(vert_taps)
    shaped = zonal.reshape(LAT, NLON, FIELDS, LEV)
    mixed = jnp.einsum("aifm,mk->aifk", shaped.astype(jnp.float32), band.astype(jnp.float32))
    return mixed.reshape(LAT, NLON, FIELDS * LEV).astype(jnp.bfloat16)
```

```python
import functools

import jax
import jax.numpy as jnp
from jax import lax
from jax.experimental import pallas as pl
from jax.experimental.pallas import tpu as pltpu
from jax.sharding import PartitionSpec as P

LEV = 64
TAPS = 15
LANES = 128


def band_of(taps_ref, columns):
    half = (TAPS - 1) // 2
    upper = lax.broadcasted_iota(jnp.int32, (columns, columns), 0)
    lower = lax.broadcasted_iota(jnp.int32, (columns, columns), 1)
    offset = upper - lower
    offset = jnp.where(upper // LEV == lower // LEV, offset, TAPS)
    band = jnp.zeros((columns, columns), jnp.float32)
    for tap in range(TAPS):
        band = jnp.where(offset == tap - half, taps_ref[tap], band)
    return band.astype(jnp.bfloat16)


def filter_kernel(taps_ref, coef_ref, x_ref, o_ref, toeplitz, band):
    parts, _, count, columns = x_ref.shape
    n = parts * count
    wide = toeplitz.shape[1]
    blocks = n // wide

    @pl.when(pl.program_id(0) == 0)
    def _():
        band[...] = band_of(taps_ref, columns)

    row = coef_ref[0].astype(jnp.float32)
    rolled = pltpu.roll(
        jnp.broadcast_to(row, (LANES, n)), 0, 1, stride=1, stride_axis=0
    )
    first = rolled.T.astype(jnp.bfloat16)
    toeplitz[:, :LANES] = first
    toeplitz[LANES:, LANES:] = first[: n - LANES]
    toeplitz[:LANES, LANES:] = first[n - LANES :]

    x = x_ref[...].reshape(n, columns)
    out = []
    for i in range(blocks):
        total = jnp.zeros((wide, columns), jnp.float32)
        for j in range(blocks):
            q = (i - j) % blocks
            total += jnp.dot(
                toeplitz[q * wide : (q + 1) * wide],
                x[j * wide : (j + 1) * wide],
                preferred_element_type=jnp.float32,
            )
        zonal = total.astype(jnp.bfloat16)
        mixed = jnp.dot(zonal, band[...], preferred_element_type=jnp.float32)
        out.append(mixed.astype(jnp.bfloat16))
    o_ref[...] = jnp.concatenate(out, axis=0).reshape(x_ref.shape)


def filtered(taps, coef, x):
    parts, lats, count, columns = x.shape
    n = parts * count
    wide = 2 * LANES
    block = pl.BlockSpec((parts, 1, count, columns), lambda a: (0, a, 0, 0))
    return pl.pallas_call(
        filter_kernel,
        grid=(lats,),
        in_specs=[
            pl.BlockSpec(memory_space=pltpu.SMEM),
            pl.BlockSpec((1, 1, n), lambda a: (a, 0, 0)),
            block,
        ],
        out_specs=block,
        out_shape=jax.ShapeDtypeStruct(x.shape, jnp.bfloat16),
        scratch_shapes=[
            pltpu.VMEM((n, wide), jnp.bfloat16),
            pltpu.VMEM((columns, columns), jnp.bfloat16),
        ],
        compiler_params=pltpu.CompilerParams(vmem_limit_bytes=32 * 1024 * 1024),
        cost_estimate=pl.CostEstimate(
            flops=2 * lats * n * (n + columns) * columns,
            bytes_accessed=4 * lats * n * columns,
            transcendentals=0,
        ),
    )(taps, coef, x)


def shards(fields, zonal_coef, vert_taps, *, parts):
    lat_rows, count, columns = fields.shape
    lats = lat_rows // parts
    me = lax.axis_index("lon")
    taps = vert_taps.astype(jnp.float32)
    coef = lax.dynamic_slice_in_dim(zonal_coef, me * lats, lats, 0)[:, None, :]
    mine = lax.all_to_all(fields, "lon", 0, 0, tiled=True)
    done = filtered(taps, coef, mine.reshape(parts, lats, count, columns))
    return lax.all_to_all(done.reshape(fields.shape), "lon", 0, 0, tiled=True)


def solution(mesh):
    placed = (P("grp", "lon", None), P(), P())
    return jax.shard_map(
        functools.partial(shards, parts=mesh.shape["lon"]),
        mesh=mesh,
        in_specs=placed,
        out_specs=P("grp", "lon", None),
        check_vma=False,
    )
```

```python
import functools

import jax
import jax.numpy as jnp
from jax import lax
from jax.experimental import pallas as pl
from jax.experimental.pallas import tpu as pltpu
from jax.sharding import PartitionSpec as P

LEV = 64
TAPS = 15
LANES = 128
WIDE = 256
STEPS = 2
VMEM = pl.BlockSpec(memory_space=pltpu.VMEM)
SMEM = pl.BlockSpec(memory_space=pltpu.SMEM)
PARAMS = pltpu.CompilerParams(vmem_limit_bytes=32 * 1024 * 1024)


def circulant_kernel(coef_ref, circ_ref):
    lats, n = coef_ref.shape
    for a in range(lats):
        row = coef_ref[a : a + 1].astype(jnp.float32)
        rolled = pltpu.roll(
            jnp.broadcast_to(row, (LANES, n)), 0, 1, stride=1, stride_axis=0
        )
        first = rolled.T.astype(jnp.bfloat16)
        circ_ref[a, :, :LANES] = first
        circ_ref[a, LANES:, LANES:] = first[: n - LANES]
        circ_ref[a, :LANES, LANES:] = first[n - LANES :]


def circulant(coef):
    lats, n = coef.shape
    return pl.pallas_call(
        circulant_kernel,
        in_specs=[VMEM],
        out_specs=VMEM,
        out_shape=jax.ShapeDtypeStruct((lats, n, WIDE), jnp.bfloat16),
        compiler_params=PARAMS,
        cost_estimate=pl.CostEstimate(
            flops=16 * lats * n * LANES, bytes_accessed=2 * lats * n * WIDE, transcendentals=0
        ),
    )(coef)


def zonal_kernel(circ_ref, x_ref, o_ref):
    parts, lats, count, columns = x_ref.shape
    n = parts * count
    for a in range(lats):
        x = x_ref[:, a].reshape(n, columns)
        first = circ_ref[a]
        circ = jnp.concatenate(
            [first] + [jnp.concatenate([first[n - j :], first[: n - j]]) for j in range(WIDE, n, WIDE)],
            axis=1,
        )
        total = jnp.dot(circ, x, preferred_element_type=jnp.float32)
        o_ref[:, a] = total.astype(jnp.bfloat16).reshape(parts, count, columns)


def zonal(circ, x):
    parts, lats, count, columns = x.shape
    n = parts * count
    return pl.pallas_call(
        zonal_kernel,
        in_specs=[VMEM, VMEM],
        out_specs=VMEM,
        out_shape=jax.ShapeDtypeStruct(x.shape, jnp.bfloat16),
        compiler_params=PARAMS,
        cost_estimate=pl.CostEstimate(
            flops=2 * lats * n * n * columns, bytes_accessed=2 * lats * n * n, transcendentals=0
        ),
    )(circ, x)


def band_kernel(taps_ref, band_ref):
    half = (TAPS - 1) // 2
    upper = lax.broadcasted_iota(jnp.int32, band_ref.shape, 0)
    lower = lax.broadcasted_iota(jnp.int32, band_ref.shape, 1)
    offset = jnp.where(upper // LEV == lower // LEV, upper - lower, TAPS)
    band = jnp.zeros(band_ref.shape, jnp.float32)
    for tap in range(TAPS):
        band = jnp.where(offset == tap - half, taps_ref[tap], band)
    band_ref[...] = band.astype(jnp.bfloat16)


def band_matrix(taps, columns):
    return pl.pallas_call(
        band_kernel,
        in_specs=[SMEM],
        out_specs=VMEM,
        out_shape=jax.ShapeDtypeStruct((columns, columns), jnp.bfloat16),
        compiler_params=PARAMS,
    )(taps)


def vertical_kernel(band_ref, x_ref, o_ref):
    rows, count, columns = o_ref.shape
    x = x_ref[pl.ds(pl.program_id(0) * rows, rows)].reshape(rows * count, columns)
    mixed = jnp.dot(x, band_ref[...], preferred_element_type=jnp.float32)
    o_ref[...] = mixed.astype(jnp.bfloat16).reshape(o_ref.shape)


def vertical(band, x):
    lat_rows, count, columns = x.shape
    rows = lat_rows // STEPS
    return pl.pallas_call(
        vertical_kernel,
        grid=(STEPS,),
        in_specs=[VMEM, VMEM],
        out_specs=pl.BlockSpec((rows, count, columns), lambda i: (i, 0, 0)),
        out_shape=jax.ShapeDtypeStruct(x.shape, jnp.bfloat16),
        compiler_params=PARAMS,
        cost_estimate=pl.CostEstimate(
            flops=2 * x.size * columns, bytes_accessed=4 * x.size, transcendentals=0
        ),
    )(band, x)


def shards(fields, zonal_coef, vert_taps, *, parts):
    lat_rows, count, columns = fields.shape
    lats = lat_rows // parts
    me = lax.axis_index("lon")
    swapped = lambda x: lax.all_to_all(x, "lon", 0, 0, tiled=True)
    circ = circulant(lax.dynamic_slice_in_dim(zonal_coef, me * lats, lats, 0))
    mine = swapped(fields).reshape(parts, lats, count, columns)
    done = zonal(circ, mine)
    done, taps = lax.optimization_barrier((done, vert_taps.astype(jnp.float32)))
    band = band_matrix(taps, columns)
    return vertical(band, swapped(done.reshape(fields.shape)))


def solution(mesh):
    placed = (P("grp", "lon", None), P(), P())
    return jax.shard_map(
        functools.partial(shards, parts=mesh.shape["lon"]),
        mesh=mesh,
        in_specs=placed,
        out_specs=P("grp", "lon", None),
        check_vma=False,
    )
```

```python
import functools

import jax
import jax.numpy as jnp
from jax import lax
from jax.experimental import pallas as pl
from jax.experimental.pallas import tpu as pltpu
from jax.sharding import PartitionSpec as P

LEV = 64
TAPS = 15
LANES = 128
WIDE = 256
STEPS = 2
NEAR = 4
HBM = pl.BlockSpec(memory_space=pltpu.HBM)
VMEM = pl.BlockSpec(memory_space=pltpu.VMEM)
SMEM = pl.BlockSpec(memory_space=pltpu.SMEM)
PARAMS = pltpu.CompilerParams(vmem_limit_bytes=32 * 1024 * 1024)


def circulant_kernel(coef_ref, circ_ref):
    lats, n = coef_ref.shape
    for a in range(lats):
        row = coef_ref[a : a + 1].astype(jnp.float32)
        rolled = pltpu.roll(
            jnp.broadcast_to(row, (LANES, n)), 0, 1, stride=1, stride_axis=0
        )
        first = rolled.T.astype(jnp.bfloat16)
        circ_ref[a, :, :LANES] = first
        circ_ref[a, LANES:, LANES:] = first[: n - LANES]
        circ_ref[a, :LANES, LANES:] = first[n - LANES :]


def circulant(coef):
    lats, n = coef.shape
    return pl.pallas_call(
        circulant_kernel,
        in_specs=[VMEM],
        out_specs=VMEM,
        out_shape=jax.ShapeDtypeStruct((lats, n, WIDE), jnp.bfloat16),
        compiler_params=PARAMS,
        cost_estimate=pl.CostEstimate(
            flops=16 * lats * n * LANES, bytes_accessed=2 * lats * n * WIDE, transcendentals=0
        ),
    )(coef)


def zonal_kernel(circ_ref, x_ref, o_ref):
    parts, lats, count, columns = x_ref.shape
    n = parts * count
    for a in range(lats):
        x = x_ref[:, a].reshape(n, columns)
        first = circ_ref[a]
        circ = jnp.concatenate(
            [first] + [jnp.concatenate([first[n - j :], first[: n - j]]) for j in range(WIDE, n, WIDE)],
            axis=1,
        )
        total = jnp.dot(circ, x, preferred_element_type=jnp.float32)
        o_ref[:, a] = total.astype(jnp.bfloat16).reshape(parts, count, columns)


def zonal(circ, x):
    parts, lats, count, columns = x.shape
    n = parts * count
    return pl.pallas_call(
        zonal_kernel,
        in_specs=[VMEM, VMEM],
        out_specs=VMEM,
        out_shape=jax.ShapeDtypeStruct(x.shape, jnp.bfloat16),
        compiler_params=PARAMS,
        cost_estimate=pl.CostEstimate(
            flops=2 * lats * n * n * columns, bytes_accessed=2 * lats * n * n, transcendentals=0
        ),
    )(circ, x)


def band_kernel(taps_ref, band_ref):
    half = (TAPS - 1) // 2
    upper = lax.broadcasted_iota(jnp.int32, band_ref.shape, 0)
    lower = lax.broadcasted_iota(jnp.int32, band_ref.shape, 1)
    offset = jnp.where(upper // LEV == lower // LEV, upper - lower, TAPS)
    band = jnp.zeros(band_ref.shape, jnp.float32)
    for tap in range(TAPS):
        band = jnp.where(offset == tap - half, taps_ref[tap], band)
    band_ref[...] = band.astype(jnp.bfloat16)


def band_matrix(taps, columns):
    return pl.pallas_call(
        band_kernel,
        in_specs=[SMEM],
        out_specs=VMEM,
        out_shape=jax.ShapeDtypeStruct((columns, columns), jnp.bfloat16),
        compiler_params=PARAMS,
    )(taps)


def vertical_kernel(band_ref, x_ref, o_ref):
    rows, count, columns = o_ref.shape
    x = x_ref[pl.ds(pl.program_id(0) * rows, rows)].reshape(rows * count, columns)
    mixed = jnp.dot(x, band_ref[...], preferred_element_type=jnp.float32)
    o_ref[...] = mixed.astype(jnp.bfloat16).reshape(o_ref.shape)


def vertical(band, x):
    lat_rows, count, columns = x.shape
    rows = lat_rows // STEPS
    return pl.pallas_call(
        vertical_kernel,
        grid=(STEPS,),
        in_specs=[VMEM, VMEM],
        out_specs=pl.BlockSpec((rows, count, columns), lambda i: (i, 0, 0)),
        out_shape=jax.ShapeDtypeStruct(x.shape, jnp.bfloat16),
        compiler_params=PARAMS,
        cost_estimate=pl.CostEstimate(
            flops=2 * x.size * columns, bytes_accessed=4 * x.size, transcendentals=0
        ),
    )(band, x)


def copied(copies):
    for copy in copies:
        copy.start()
    for copy in copies:
        copy.wait()


def first_half_kernel(x_ref, o_ref, sem):
    copied([pltpu.make_async_copy(x_ref.at[pl.ds(0, o_ref.shape[0])], o_ref, sem.at[0])])


def first_half(x):
    lat_rows, count, columns = x.shape
    return pl.pallas_call(
        first_half_kernel,
        in_specs=[HBM],
        out_specs=VMEM,
        out_shape=jax.ShapeDtypeStruct((lat_rows // 2, count, columns), jnp.bfloat16),
        scratch_shapes=[pltpu.SemaphoreType.DMA((1,))],
        compiler_params=PARAMS,
    )(x)


def second_half_kernel(me_ref, x_ref, *refs):
    outs, sem = refs[:-1], refs[-1]
    half = len(outs) * NEAR
    copies = []
    for r in range(half):
        x = x_ref.at[half + (me_ref[0] ^ r)]
        out = outs[r // NEAR].at[r % NEAR]
        copies.append(pltpu.make_async_copy(x, out, sem.at[r]))
    copied(copies)


def second_half(me, x):
    lat_rows, count, columns = x.shape
    arrays = lat_rows // 2 // NEAR
    return pl.pallas_call(
        second_half_kernel,
        in_specs=[SMEM, HBM],
        out_specs=[VMEM] * arrays,
        out_shape=[jax.ShapeDtypeStruct((NEAR, count, columns), jnp.bfloat16)] * arrays,
        scratch_shapes=[pltpu.SemaphoreType.DMA((lat_rows // 2,))],
        compiler_params=PARAMS,
    )(me, x)


def rotations(first):
    n, wide = first.shape
    turned = [jnp.concatenate([first[n - j :], first[: n - j]]) for j in range(wide, n, wide)]
    return jnp.concatenate([first] + turned, axis=1)


def zonal_first_kernel(circ_ref, x_ref, o_ref):
    parts, count, columns = x_ref.shape
    x = x_ref[...].reshape(parts * count, columns)
    total = jnp.dot(rotations(circ_ref[0]), x, preferred_element_type=jnp.float32)
    o_ref[...] = total.astype(jnp.bfloat16).reshape(o_ref.shape)


def zonal_cost(circ, columns):
    n = circ.shape[1]
    return pl.CostEstimate(
        flops=2 * n * n * columns, bytes_accessed=2 * n * n, transcendentals=0
    )


def zonal_first(circ, x):
    return pl.pallas_call(
        zonal_first_kernel,
        in_specs=[VMEM, VMEM],
        out_specs=VMEM,
        out_shape=jax.ShapeDtypeStruct(x.shape, jnp.bfloat16),
        compiler_params=PARAMS,
        cost_estimate=zonal_cost(circ, x.shape[2]),
    )(circ, x)


def distance_of(core, i, far):
    return i % far * NEAR + i // far * 2 + core


def zonal_second_kernel(me_ref, circ_ref, *refs):
    ins, outs, (x, z) = refs[:2], refs[2:-2], refs[-2:]
    parts, count, columns = x.shape
    for core in range(2):
        for i in range(parts // 2):
            r = distance_of(core, i, len(outs))
            x[me_ref[0] ^ r] = ins[core][i]
    total = jnp.dot(
        rotations(circ_ref[1]),
        x[...].reshape(parts * count, columns),
        preferred_element_type=jnp.float32,
    )
    z[...] = total.astype(jnp.bfloat16).reshape(z.shape)
    for r in range(parts):
        outs[r // NEAR][r % NEAR] = z[me_ref[0] ^ r]


def zonal_second(me, circ, blocks):
    half, count, columns = blocks[0].shape
    arrays = 2 * half // NEAR
    return pl.pallas_call(
        zonal_second_kernel,
        in_specs=[SMEM] + [VMEM] * 3,
        out_specs=[VMEM] * arrays,
        out_shape=[jax.ShapeDtypeStruct((NEAR, count, columns), jnp.bfloat16)] * arrays,
        scratch_shapes=[pltpu.VMEM((2 * half, count, columns), jnp.bfloat16)] * 2,
        compiler_params=PARAMS,
        cost_estimate=zonal_cost(circ, columns),
    )(me, circ, *blocks)


def vertical_first_kernel(band_ref, x_ref, _, o_ref):
    x = x_ref[...].reshape(-1, x_ref.shape[2])
    mixed = jnp.dot(x, band_ref[...], preferred_element_type=jnp.float32)
    o_ref[...] = mixed.astype(jnp.bfloat16).reshape(o_ref.shape)


def vertical_first(band, x, result):
    parts, count, columns = x.shape
    rows = parts // STEPS
    return pl.pallas_call(
        vertical_first_kernel,
        grid=(STEPS,),
        in_specs=[VMEM, pl.BlockSpec((rows, count, columns), lambda i: (i, 0, 0)), HBM],
        out_specs=pl.BlockSpec((rows, count, columns), lambda i: (i, 0, 0)),
        out_shape=jax.ShapeDtypeStruct(result.shape, jnp.bfloat16),
        input_output_aliases={2: 0},
        compiler_params=PARAMS,
    )(band, x, result)


def vertical_second_kernel(me_ref, band_ref, *refs):
    ins, (o_ref, mixed, sem) = refs[:2], refs[2:]
    parts, count, columns = mixed.shape
    half = parts // 2
    copies = []
    for core in range(2):
        x = ins[core][...].reshape(half * count, columns)
        out = jnp.dot(x, band_ref[...], preferred_element_type=jnp.float32)
        out = out.astype(jnp.bfloat16).reshape(ins[core].shape)
        mixed[core * half : (core + 1) * half] = out
        for i in range(half):
            lat = parts + (me_ref[0] ^ distance_of(core, i, parts // NEAR))
            block = core * half + i
            copy = pltpu.make_async_copy(mixed.at[block], o_ref.at[lat], sem.at[block])
            copy.start()
            copies.append(copy)
    for copy in copies:
        copy.wait()


def vertical_second(me, band, blocks):
    half, count, columns = blocks[0].shape
    return pl.pallas_call(
        vertical_second_kernel,
        in_specs=[SMEM] + [VMEM] * 3,
        out_specs=HBM,
        out_shape=jax.ShapeDtypeStruct((4 * half, count, columns), jnp.bfloat16),
        scratch_shapes=[
            pltpu.VMEM((2 * half, count, columns), jnp.bfloat16),
            pltpu.SemaphoreType.DMA((2 * half,)),
        ],
        compiler_params=PARAMS,
    )(me, band, *blocks)


def hop(x, distance, parts):
    return lax.ppermute(x, "lon", [(i, i ^ distance) for i in range(parts)])


def far_hops(arrays, parts):
    return [arrays[0]] + [hop(arrays[i], i * NEAR, parts) for i in range(1, len(arrays))]


def near_hops(arrays, parts):
    far, shape = len(arrays), arrays[0].shape[1:]
    state = jnp.stack(arrays).reshape((far, 2, 2) + shape)
    state = jnp.stack([state[:, 0], hop(state[:, 1], 2, parts)])
    keep, send = (state[:, :, i].reshape((2 * far,) + shape) for i in range(2))
    return keep, hop(send, 1, parts)


def two_ways(fields, zonal_coef, vert_taps, parts):
    lat_rows, count, columns = fields.shape
    position = lax.axis_index("lon")
    me = position.reshape(1)
    swapped = lambda x: lax.all_to_all(x, "lon", 0, 0, tiled=True)
    band = band_matrix(vert_taps.astype(jnp.float32), columns)
    coef = lax.dynamic_index_in_dim(
        zonal_coef.reshape(2, parts, -1), position, 1, keepdims=False
    )
    circ = circulant(coef)
    arrays = far_hops(second_half(me, fields), parts)
    x = first_half(fields)
    x, _ = lax.optimization_barrier((x, [arrays[3]]))
    mine = swapped(x)
    arrays = near_hops(arrays, parts)
    arrays = zonal_second(me, circ, arrays)
    mine, _ = lax.optimization_barrier((mine, arrays[0]))
    arrays = far_hops(arrays, parts)
    done = zonal_first(circ, mine)
    _, *after = lax.optimization_barrier((done, *arrays))
    done, _ = lax.optimization_barrier((done, [arrays[3]]))
    back = swapped(done)
    result = vertical_second(me, band, near_hops(after, parts))
    back, result = lax.optimization_barrier((back, result))
    return vertical_first(band, back, result)


def shards(fields, zonal_coef, vert_taps, *, parts):
    lat_rows, count, columns = fields.shape
    lats = lat_rows // parts
    if lats == 2 and parts & (parts - 1) == 0 and parts >= NEAR:
        return two_ways(fields, zonal_coef, vert_taps, parts)
    me = lax.axis_index("lon")
    swapped = lambda x: lax.all_to_all(x, "lon", 0, 0, tiled=True)
    circ = circulant(lax.dynamic_slice_in_dim(zonal_coef, me * lats, lats, 0))
    mine = swapped(fields).reshape(parts, lats, count, columns)
    done = zonal(circ, mine)
    done, taps = lax.optimization_barrier((done, vert_taps.astype(jnp.float32)))
    band = band_matrix(taps, columns)
    return vertical(band, swapped(done.reshape(fields.shape)))


def solution(mesh):
    placed = (P("grp", "lon", None), P(), P())
    return jax.shard_map(
        functools.partial(shards, parts=mesh.shape["lon"]),
        mesh=mesh,
        in_specs=placed,
        out_specs=P("grp", "lon", None),
        check_vma=False,
    )
```

```python
import functools

import jax
import jax.numpy as jnp
from jax import lax
from jax.experimental import pallas as pl
from jax.experimental.pallas import tpu as pltpu
from jax.sharding import PartitionSpec as P

LEV = 64
TAPS = 15
LANES = 128
WIDE = 256
STEPS = 2
NEAR = 4
HBM = pl.BlockSpec(memory_space=pltpu.HBM)
VMEM = pl.BlockSpec(memory_space=pltpu.VMEM)
SMEM = pl.BlockSpec(memory_space=pltpu.SMEM)
PARAMS = pltpu.CompilerParams(vmem_limit_bytes=32 * 1024 * 1024)


def circulant_kernel(coef_ref, circ_ref):
    lats, n = coef_ref.shape
    for a in range(lats):
        row = coef_ref[a : a + 1].astype(jnp.float32)
        rolled = pltpu.roll(
            jnp.broadcast_to(row, (LANES, n)), 0, 1, stride=1, stride_axis=0
        )
        first = rolled.T.astype(jnp.bfloat16)
        circ_ref[a, :, :LANES] = first
        circ_ref[a, LANES:, LANES:] = first[: n - LANES]
        circ_ref[a, :LANES, LANES:] = first[n - LANES :]


def circulant(coef):
    lats, n = coef.shape
    return pl.pallas_call(
        circulant_kernel,
        in_specs=[VMEM],
        out_specs=VMEM,
        out_shape=jax.ShapeDtypeStruct((lats, n, WIDE), jnp.bfloat16),
        compiler_params=PARAMS,
        cost_estimate=pl.CostEstimate(
            flops=16 * lats * n * LANES, bytes_accessed=2 * lats * n * WIDE, transcendentals=0
        ),
    )(coef)


def zonal_kernel(circ_ref, x_ref, o_ref):
    parts, lats, count, columns = x_ref.shape
    n = parts * count
    for a in range(lats):
        x = x_ref[:, a].reshape(n, columns)
        first = circ_ref[a]
        circ = jnp.concatenate(
            [first] + [jnp.concatenate([first[n - j :], first[: n - j]]) for j in range(WIDE, n, WIDE)],
            axis=1,
        )
        total = jnp.dot(circ, x, preferred_element_type=jnp.float32)
        o_ref[:, a] = total.astype(jnp.bfloat16).reshape(parts, count, columns)


def zonal(circ, x):
    parts, lats, count, columns = x.shape
    n = parts * count
    return pl.pallas_call(
        zonal_kernel,
        in_specs=[VMEM, VMEM],
        out_specs=VMEM,
        out_shape=jax.ShapeDtypeStruct(x.shape, jnp.bfloat16),
        compiler_params=PARAMS,
        cost_estimate=pl.CostEstimate(
            flops=2 * lats * n * n * columns, bytes_accessed=2 * lats * n * n, transcendentals=0
        ),
    )(circ, x)


def band_kernel(taps_ref, band_ref):
    half = (TAPS - 1) // 2
    upper = lax.broadcasted_iota(jnp.int32, band_ref.shape, 0)
    lower = lax.broadcasted_iota(jnp.int32, band_ref.shape, 1)
    offset = jnp.where(upper // LEV == lower // LEV, upper - lower, TAPS)
    band = jnp.zeros(band_ref.shape, jnp.float32)
    for tap in range(TAPS):
        band = jnp.where(offset == tap - half, taps_ref[tap], band)
    band_ref[...] = band.astype(jnp.bfloat16)


def band_matrix(taps, columns):
    return pl.pallas_call(
        band_kernel,
        in_specs=[SMEM],
        out_specs=VMEM,
        out_shape=jax.ShapeDtypeStruct((columns, columns), jnp.bfloat16),
        compiler_params=PARAMS,
    )(taps)


def vertical_kernel(band_ref, x_ref, o_ref):
    rows, count, columns = o_ref.shape
    x = x_ref[pl.ds(pl.program_id(0) * rows, rows)].reshape(rows * count, columns)
    mixed = jnp.dot(x, band_ref[...], preferred_element_type=jnp.float32)
    o_ref[...] = mixed.astype(jnp.bfloat16).reshape(o_ref.shape)


def vertical(band, x):
    lat_rows, count, columns = x.shape
    rows = lat_rows // STEPS
    return pl.pallas_call(
        vertical_kernel,
        grid=(STEPS,),
        in_specs=[VMEM, VMEM],
        out_specs=pl.BlockSpec((rows, count, columns), lambda i: (i, 0, 0)),
        out_shape=jax.ShapeDtypeStruct(x.shape, jnp.bfloat16),
        compiler_params=PARAMS,
        cost_estimate=pl.CostEstimate(
            flops=2 * x.size * columns, bytes_accessed=4 * x.size, transcendentals=0
        ),
    )(band, x)


def copied(copies):
    for copy in copies:
        copy.start()
    for copy in copies:
        copy.wait()


def first_half_kernel(x_ref, o_ref, sem):
    copied([pltpu.make_async_copy(x_ref.at[pl.ds(0, o_ref.shape[0])], o_ref, sem.at[0])])


def first_half(x):
    lat_rows, count, columns = x.shape
    return pl.pallas_call(
        first_half_kernel,
        in_specs=[HBM],
        out_specs=VMEM,
        out_shape=jax.ShapeDtypeStruct((lat_rows // 2, count, columns), jnp.bfloat16),
        scratch_shapes=[pltpu.SemaphoreType.DMA((1,))],
        compiler_params=PARAMS,
    )(x)


def second_half_kernel(me_ref, x_ref, *refs):
    outs, sem = refs[:-1], refs[-1]
    half = len(outs) * NEAR
    copies = []
    for r in range(half):
        x = x_ref.at[half + (me_ref[0] ^ r)]
        out = outs[r // NEAR].at[r % NEAR]
        copies.append(pltpu.make_async_copy(x, out, sem.at[r]))
    copied(copies)


def second_half(me, x):
    lat_rows, count, columns = x.shape
    arrays = lat_rows // 2 // NEAR
    return pl.pallas_call(
        second_half_kernel,
        in_specs=[SMEM, HBM],
        out_specs=[VMEM] * arrays,
        out_shape=[jax.ShapeDtypeStruct((NEAR, count, columns), jnp.bfloat16)] * arrays,
        scratch_shapes=[pltpu.SemaphoreType.DMA((lat_rows // 2,))],
        compiler_params=PARAMS,
    )(me, x)


def rotations(first):
    n, wide = first.shape
    turned = [jnp.concatenate([first[n - j :], first[: n - j]]) for j in range(wide, n, wide)]
    return jnp.concatenate([first] + turned, axis=1)


def zonal_first_kernel(circ_ref, x_ref, o_ref):
    parts, count, columns = x_ref.shape
    x = x_ref[...].reshape(parts * count, columns)
    total = jnp.dot(rotations(circ_ref[0]), x, preferred_element_type=jnp.float32)
    o_ref[...] = total.astype(jnp.bfloat16).reshape(o_ref.shape)


def zonal_cost(circ, columns):
    n = circ.shape[1]
    return pl.CostEstimate(
        flops=2 * n * n * columns, bytes_accessed=2 * n * n, transcendentals=0
    )


def zonal_first(circ, x):
    return pl.pallas_call(
        zonal_first_kernel,
        in_specs=[VMEM, VMEM],
        out_specs=VMEM,
        out_shape=jax.ShapeDtypeStruct(x.shape, jnp.bfloat16),
        compiler_params=PARAMS,
        cost_estimate=zonal_cost(circ, x.shape[2]),
    )(circ, x)


def distance_of(core, i, far):
    return i % far * NEAR + i // far * 2 + core


def zonal_second_kernel(me_ref, circ_ref, *refs):
    ins, outs, (x, z) = refs[:2], refs[2:-2], refs[-2:]
    parts, count, columns = x.shape
    for core in range(2):
        for i in range(parts // 2):
            r = distance_of(core, i, len(outs))
            x[me_ref[0] ^ r] = ins[core][i]
    total = jnp.dot(
        rotations(circ_ref[1]),
        x[...].reshape(parts * count, columns),
        preferred_element_type=jnp.float32,
    )
    z[...] = total.astype(jnp.bfloat16).reshape(z.shape)
    for r in range(parts):
        outs[r // NEAR][r % NEAR] = z[me_ref[0] ^ r]


def zonal_second(me, circ, blocks):
    half, count, columns = blocks[0].shape
    arrays = 2 * half // NEAR
    return pl.pallas_call(
        zonal_second_kernel,
        in_specs=[SMEM] + [VMEM] * 3,
        out_specs=[VMEM] * arrays,
        out_shape=[jax.ShapeDtypeStruct((NEAR, count, columns), jnp.bfloat16)] * arrays,
        scratch_shapes=[pltpu.VMEM((2 * half, count, columns), jnp.bfloat16)] * 2,
        compiler_params=PARAMS,
        cost_estimate=zonal_cost(circ, columns),
    )(me, circ, *blocks)


def vertical_first_kernel(band_ref, x_ref, o_ref):
    x = x_ref[...].reshape(-1, x_ref.shape[2])
    mixed = jnp.dot(x, band_ref[...], preferred_element_type=jnp.float32)
    o_ref[...] = mixed.astype(jnp.bfloat16).reshape(o_ref.shape)


def vertical_first(band, x):
    parts, count, columns = x.shape
    rows = parts // STEPS
    return pl.pallas_call(
        vertical_first_kernel,
        grid=(STEPS,),
        in_specs=[VMEM, pl.BlockSpec((rows, count, columns), lambda i: (i, 0, 0))],
        out_specs=pl.BlockSpec((rows, count, columns), lambda i: (i, 0, 0)),
        out_shape=jax.ShapeDtypeStruct((2 * parts, count, columns), jnp.bfloat16),
        compiler_params=PARAMS,
    )(band, x)


def vertical_second_kernel(me_ref, band_ref, *refs):
    ins, (o_ref, mixed, sem) = refs[:2], refs[3:]
    parts, count, columns = mixed.shape
    half = parts // 2
    copies = []
    for core in range(2):
        x = ins[core][...].reshape(half * count, columns)
        out = jnp.dot(x, band_ref[...], preferred_element_type=jnp.float32)
        out = out.astype(jnp.bfloat16).reshape(ins[core].shape)
        mixed[core * half : (core + 1) * half] = out
        for i in range(half):
            lat = parts + (me_ref[0] ^ distance_of(core, i, parts // NEAR))
            block = core * half + i
            copy = pltpu.make_async_copy(mixed.at[block], o_ref.at[lat], sem.at[block])
            copy.start()
            copies.append(copy)
    for copy in copies:
        copy.wait()


def vertical_second(me, band, blocks, result):
    half, count, columns = blocks[0].shape
    return pl.pallas_call(
        vertical_second_kernel,
        in_specs=[SMEM] + [VMEM] * 3 + [HBM],
        out_specs=HBM,
        out_shape=jax.ShapeDtypeStruct((4 * half, count, columns), jnp.bfloat16),
        scratch_shapes=[
            pltpu.VMEM((2 * half, count, columns), jnp.bfloat16),
            pltpu.SemaphoreType.DMA((2 * half,)),
        ],
        input_output_aliases={4: 0},
        compiler_params=PARAMS,
    )(me, band, *blocks, result)


def hop(x, distance, parts):
    return lax.ppermute(x, "lon", [(i, i ^ distance) for i in range(parts)])


def far_hops(arrays, parts):
    return [arrays[0]] + [hop(arrays[i], i * NEAR, parts) for i in range(1, len(arrays))]


def near_hops(arrays, parts):
    far, shape = len(arrays), arrays[0].shape[1:]
    state = jnp.stack(arrays).reshape((far, 2, 2) + shape)
    state = jnp.stack([state[:, 0], hop(state[:, 1], 2, parts)])
    keep, send = (state[:, :, i].reshape((2 * far,) + shape) for i in range(2))
    return keep, hop(send, 1, parts)


def two_ways(fields, zonal_coef, vert_taps, parts):
    lat_rows, count, columns = fields.shape
    position = lax.axis_index("lon")
    me = position.reshape(1)
    swapped = lambda x: lax.all_to_all(x, "lon", 0, 0, tiled=True)
    band = band_matrix(vert_taps.astype(jnp.float32), columns)
    coef = lax.dynamic_index_in_dim(
        zonal_coef.reshape(2, parts, -1), position, 1, keepdims=False
    )
    circ = circulant(coef)
    arrays = far_hops(second_half(me, fields), parts)
    x = first_half(fields)
    x, _ = lax.optimization_barrier((x, [arrays[1]]))
    mine = swapped(x)
    arrays = near_hops(arrays, parts)
    arrays = zonal_second(me, circ, arrays)
    mine, _ = lax.optimization_barrier((mine, arrays[0]))
    arrays = far_hops(arrays, parts)
    done = zonal_first(circ, mine)
    _, *after = lax.optimization_barrier((done, *arrays))
    done, _ = lax.optimization_barrier((done, [arrays[3]]))
    back = swapped(done)
    blocks = near_hops(after, parts)
    return vertical_second(me, band, blocks, vertical_first(band, back))


def shards(fields, zonal_coef, vert_taps, *, parts):
    lat_rows, count, columns = fields.shape
    lats = lat_rows // parts
    if lats == 2 and parts & (parts - 1) == 0 and parts >= NEAR:
        return two_ways(fields, zonal_coef, vert_taps, parts)
    me = lax.axis_index("lon")
    swapped = lambda x: lax.all_to_all(x, "lon", 0, 0, tiled=True)
    circ = circulant(lax.dynamic_slice_in_dim(zonal_coef, me * lats, lats, 0))
    mine = swapped(fields).reshape(parts, lats, count, columns)
    done = zonal(circ, mine)
    done, taps = lax.optimization_barrier((done, vert_taps.astype(jnp.float32)))
    band = band_matrix(taps, columns)
    return vertical(band, swapped(done.reshape(fields.shape)))


def solution(mesh):
    placed = (P("grp", "lon", None), P(), P())
    return jax.shard_map(
        functools.partial(shards, parts=mesh.shape["lon"]),
        mesh=mesh,
        in_specs=placed,
        out_specs=P("grp", "lon", None),
        check_vma=False,
    )
```

```python
import functools

import jax
import jax.numpy as jnp
from jax import lax
from jax.experimental import pallas as pl
from jax.experimental.pallas import tpu as pltpu
from jax.sharding import PartitionSpec as P

LEV = 64
TAPS = 15
LANES = 128
WIDE = 256
STEPS = 2
NEAR = 4
HBM = pl.BlockSpec(memory_space=pltpu.HBM)
VMEM = pl.BlockSpec(memory_space=pltpu.VMEM)
SMEM = pl.BlockSpec(memory_space=pltpu.SMEM)
PARAMS = pltpu.CompilerParams(vmem_limit_bytes=32 * 1024 * 1024)


def circulant_kernel(coef_ref, circ_ref):
    lats, n = coef_ref.shape
    for a in range(lats):
        row = coef_ref[a : a + 1].astype(jnp.float32)
        rolled = pltpu.roll(
            jnp.broadcast_to(row, (LANES, n)), 0, 1, stride=1, stride_axis=0
        )
        first = rolled.T.astype(jnp.bfloat16)
        circ_ref[a, :, :LANES] = first
        circ_ref[a, LANES:, LANES:] = first[: n - LANES]
        circ_ref[a, :LANES, LANES:] = first[n - LANES :]


def circulant(coef):
    lats, n = coef.shape
    return pl.pallas_call(
        circulant_kernel,
        in_specs=[VMEM],
        out_specs=VMEM,
        out_shape=jax.ShapeDtypeStruct((lats, n, WIDE), jnp.bfloat16),
        compiler_params=PARAMS,
        cost_estimate=pl.CostEstimate(
            flops=16 * lats * n * LANES, bytes_accessed=2 * lats * n * WIDE, transcendentals=0
        ),
    )(coef)


def zonal_kernel(circ_ref, x_ref, o_ref):
    parts, lats, count, columns = x_ref.shape
    n = parts * count
    for a in range(lats):
        x = x_ref[:, a].reshape(n, columns)
        first = circ_ref[a]
        circ = jnp.concatenate(
            [first] + [jnp.concatenate([first[n - j :], first[: n - j]]) for j in range(WIDE, n, WIDE)],
            axis=1,
        )
        total = jnp.dot(circ, x, preferred_element_type=jnp.float32)
        o_ref[:, a] = total.astype(jnp.bfloat16).reshape(parts, count, columns)


def zonal(circ, x):
    parts, lats, count, columns = x.shape
    n = parts * count
    return pl.pallas_call(
        zonal_kernel,
        in_specs=[VMEM, VMEM],
        out_specs=VMEM,
        out_shape=jax.ShapeDtypeStruct(x.shape, jnp.bfloat16),
        compiler_params=PARAMS,
        cost_estimate=pl.CostEstimate(
            flops=2 * lats * n * n * columns, bytes_accessed=2 * lats * n * n, transcendentals=0
        ),
    )(circ, x)


def band_kernel(taps_ref, band_ref):
    half = (TAPS - 1) // 2
    upper = lax.broadcasted_iota(jnp.int32, band_ref.shape, 0)
    lower = lax.broadcasted_iota(jnp.int32, band_ref.shape, 1)
    offset = jnp.where(upper // LEV == lower // LEV, upper - lower, TAPS)
    band = jnp.zeros(band_ref.shape, jnp.float32)
    for tap in range(TAPS):
        band = jnp.where(offset == tap - half, taps_ref[tap], band)
    band_ref[...] = band.astype(jnp.bfloat16)


def band_matrix(taps, columns):
    return pl.pallas_call(
        band_kernel,
        in_specs=[SMEM],
        out_specs=VMEM,
        out_shape=jax.ShapeDtypeStruct((columns, columns), jnp.bfloat16),
        compiler_params=PARAMS,
    )(taps)


def vertical_kernel(band_ref, x_ref, o_ref):
    rows, count, columns = o_ref.shape
    x = x_ref[pl.ds(pl.program_id(0) * rows, rows)].reshape(rows * count, columns)
    mixed = jnp.dot(x, band_ref[...], preferred_element_type=jnp.float32)
    o_ref[...] = mixed.astype(jnp.bfloat16).reshape(o_ref.shape)


def vertical(band, x):
    lat_rows, count, columns = x.shape
    rows = lat_rows // STEPS
    return pl.pallas_call(
        vertical_kernel,
        grid=(STEPS,),
        in_specs=[VMEM, VMEM],
        out_specs=pl.BlockSpec((rows, count, columns), lambda i: (i, 0, 0)),
        out_shape=jax.ShapeDtypeStruct(x.shape, jnp.bfloat16),
        compiler_params=PARAMS,
        cost_estimate=pl.CostEstimate(
            flops=2 * x.size * columns, bytes_accessed=4 * x.size, transcendentals=0
        ),
    )(band, x)


def copied(copies):
    for copy in copies:
        copy.start()
    for copy in copies:
        copy.wait()


def first_half_kernel(x_ref, o_ref, sem):
    copied([pltpu.make_async_copy(x_ref.at[pl.ds(0, o_ref.shape[0])], o_ref, sem.at[0])])


def first_half(x):
    lat_rows, count, columns = x.shape
    return pl.pallas_call(
        first_half_kernel,
        in_specs=[HBM],
        out_specs=VMEM,
        out_shape=jax.ShapeDtypeStruct((lat_rows // 2, count, columns), jnp.bfloat16),
        scratch_shapes=[pltpu.SemaphoreType.DMA((1,))],
        compiler_params=pltpu.CompilerParams(vmem_limit_bytes=61 * 1024 * 1024),
    )(x)


def second_half_kernel(first, me_ref, x_ref, *refs):
    outs, sem = refs[:-1], refs[-1]
    half = x_ref.shape[0] // 2
    copies = []
    for i in range(len(outs) * NEAR):
        x = x_ref.at[half + (me_ref[0] ^ (first * NEAR + i))]
        out = outs[i // NEAR].at[i % NEAR]
        copies.append(pltpu.make_async_copy(x, out, sem.at[i]))
    copied(copies)


def second_half(me, x, first, arrays):
    _, count, columns = x.shape
    return pl.pallas_call(
        functools.partial(second_half_kernel, first),
        in_specs=[SMEM, HBM],
        out_specs=[VMEM] * arrays,
        out_shape=[jax.ShapeDtypeStruct((NEAR, count, columns), jnp.bfloat16)] * arrays,
        scratch_shapes=[pltpu.SemaphoreType.DMA((arrays * NEAR,))],
        compiler_params=pltpu.CompilerParams(vmem_limit_bytes=61 * 1024 * 1024),
    )(me, x)


def rotations(first):
    n, wide = first.shape
    turned = [jnp.concatenate([first[n - j :], first[: n - j]]) for j in range(wide, n, wide)]
    return jnp.concatenate([first] + turned, axis=1)


def zonal_first_kernel(circ_ref, x_ref, o_ref):
    parts, count, columns = x_ref.shape
    x = x_ref[...].reshape(parts * count, columns)
    total = jnp.dot(rotations(circ_ref[0]), x, preferred_element_type=jnp.float32)
    o_ref[...] = total.astype(jnp.bfloat16).reshape(o_ref.shape)


def zonal_cost(circ, columns, times=1):
    n = circ.shape[1]
    return pl.CostEstimate(
        flops=int(times * 2 * n * n * columns), bytes_accessed=2 * n * n, transcendentals=0
    )


def zonal_first(circ, x):
    return pl.pallas_call(
        zonal_first_kernel,
        in_specs=[VMEM, VMEM],
        out_specs=VMEM,
        out_shape=jax.ShapeDtypeStruct(x.shape, jnp.bfloat16),
        compiler_params=PARAMS,
        cost_estimate=zonal_cost(circ, x.shape[2]),
    )(circ, x)


def distance_of(core, i, far):
    return i % far * NEAR + i // far * 2 + core


def zonal_second_kernel(me_ref, circ_ref, *refs):
    ins, outs, (x, z) = refs[:2], refs[2:-2], refs[-2:]
    parts, count, columns = x.shape
    for core in range(2):
        for i in range(parts // 2):
            r = distance_of(core, i, len(outs))
            x[me_ref[0] ^ r] = ins[core][i]
    total = jnp.dot(
        rotations(circ_ref[1]),
        x[...].reshape(parts * count, columns),
        preferred_element_type=jnp.float32,
    )
    z[...] = total.astype(jnp.bfloat16).reshape(z.shape)
    for r in range(parts):
        outs[r // NEAR][r % NEAR] = z[me_ref[0] ^ r]


def zonal_second(me, circ, blocks):
    half, count, columns = blocks[0].shape
    arrays = 2 * half // NEAR
    return pl.pallas_call(
        zonal_second_kernel,
        in_specs=[SMEM] + [VMEM] * 3,
        out_specs=[VMEM] * arrays,
        out_shape=[jax.ShapeDtypeStruct((NEAR, count, columns), jnp.bfloat16)] * arrays,
        scratch_shapes=[pltpu.VMEM((2 * half, count, columns), jnp.bfloat16)] * 2,
        compiler_params=PARAMS,
        cost_estimate=zonal_cost(circ, columns, 4),
    )(me, circ, *blocks)


def vertical_first_kernel(band_ref, x_ref, o_ref):
    x = x_ref[...].reshape(-1, x_ref.shape[2])
    mixed = jnp.dot(x, band_ref[...], preferred_element_type=jnp.float32)
    o_ref[...] = mixed.astype(jnp.bfloat16).reshape(o_ref.shape)


def vertical_first(band, x):
    parts, count, columns = x.shape
    rows = parts // STEPS
    return pl.pallas_call(
        vertical_first_kernel,
        grid=(STEPS,),
        in_specs=[VMEM, pl.BlockSpec((rows, count, columns), lambda i: (i, 0, 0))],
        out_specs=pl.BlockSpec((rows, count, columns), lambda i: (i, 0, 0)),
        out_shape=jax.ShapeDtypeStruct((2 * parts, count, columns), jnp.bfloat16),
        compiler_params=PARAMS,
    )(band, x)


def vertical_second_kernel(me_ref, band_ref, *refs):
    ins, (o_ref, mixed, sem) = refs[:2], refs[3:]
    parts, count, columns = mixed.shape
    half = parts // 2
    copies = []
    for core in range(2):
        x = ins[core][...].reshape(half * count, columns)
        out = jnp.dot(x, band_ref[...], preferred_element_type=jnp.float32)
        out = out.astype(jnp.bfloat16).reshape(ins[core].shape)
        mixed[core * half : (core + 1) * half] = out
        for i in range(half):
            lat = parts + (me_ref[0] ^ distance_of(core, i, parts // NEAR))
            block = core * half + i
            copy = pltpu.make_async_copy(mixed.at[block], o_ref.at[lat], sem.at[block])
            copy.start()
            copies.append(copy)
    for copy in copies:
        copy.wait()


def vertical_second(me, band, blocks, result):
    half, count, columns = blocks[0].shape
    return pl.pallas_call(
        vertical_second_kernel,
        in_specs=[SMEM] + [VMEM] * 3 + [HBM],
        out_specs=HBM,
        out_shape=jax.ShapeDtypeStruct((4 * half, count, columns), jnp.bfloat16),
        scratch_shapes=[
            pltpu.VMEM((2 * half, count, columns), jnp.bfloat16),
            pltpu.SemaphoreType.DMA((2 * half,)),
        ],
        input_output_aliases={4: 0},
        compiler_params=PARAMS,
    )(me, band, *blocks, result)


def hop(x, distance, parts):
    return lax.ppermute(x, "lon", [(i, i ^ distance) for i in range(parts)])


def far_hops(arrays, parts):
    return [arrays[0]] + [hop(arrays[i], i * NEAR, parts) for i in range(1, len(arrays))]


def near_hops(arrays, parts):
    far, shape = len(arrays), arrays[0].shape[1:]
    state = jnp.stack(arrays).reshape((far, 2, 2) + shape)
    state = jnp.stack([state[:, 0], hop(state[:, 1], 2, parts)])
    keep, send = (state[:, :, i].reshape((2 * far,) + shape) for i in range(2))
    return keep, hop(send, 1, parts)


def two_ways(fields, zonal_coef, vert_taps, parts):
    lat_rows, count, columns = fields.shape
    position = lax.axis_index("lon")
    me = position.reshape(1)
    swapped = lambda x: lax.all_to_all(x, "lon", 0, 0, tiled=True)
    band = band_matrix(vert_taps.astype(jnp.float32), columns)
    coef = lax.dynamic_index_in_dim(
        zonal_coef.reshape(2, parts, -1), position, 1, keepdims=False
    )
    circ = circulant(coef)
    far = second_half(me, fields, 1, parts // NEAR - 1)
    stays, _ = lax.optimization_barrier((fields, far[0]))
    arrays = far_hops([*second_half(me, stays, 0, 1), *far], parts)
    x = first_half(fields)
    x, _ = lax.optimization_barrier((x, [arrays[1]]))
    mine = swapped(x)
    arrays = near_hops(arrays, parts)
    arrays = zonal_second(me, circ, arrays)
    mine, _ = lax.optimization_barrier((mine, arrays[0]))
    arrays = far_hops(arrays, parts)
    done = zonal_first(circ, mine)
    _, *after = lax.optimization_barrier((done, *arrays))
    done, _ = lax.optimization_barrier((done, [arrays[3]]))
    back = swapped(done)
    blocks = near_hops(after, parts)
    return vertical_second(me, band, blocks, vertical_first(band, back))


def shards(fields, zonal_coef, vert_taps, *, parts):
    lat_rows, count, columns = fields.shape
    lats = lat_rows // parts
    if lats == 2 and parts & (parts - 1) == 0 and parts >= NEAR:
        return two_ways(fields, zonal_coef, vert_taps, parts)
    me = lax.axis_index("lon")
    swapped = lambda x: lax.all_to_all(x, "lon", 0, 0, tiled=True)
    circ = circulant(lax.dynamic_slice_in_dim(zonal_coef, me * lats, lats, 0))
    mine = swapped(fields).reshape(parts, lats, count, columns)
    done = zonal(circ, mine)
    done, taps = lax.optimization_barrier((done, vert_taps.astype(jnp.float32)))
    band = band_matrix(taps, columns)
    return vertical(band, swapped(done.reshape(fields.shape)))


def solution(mesh):
    placed = (P("grp", "lon", None), P(), P())
    return jax.shard_map(
        functools.partial(shards, parts=mesh.shape["lon"]),
        mesh=mesh,
        in_specs=placed,
        out_specs=P("grp", "lon", None),
        check_vma=False,
    )
```

```python
import functools

import jax
import jax.numpy as jnp
from jax import lax
from jax.experimental import pallas as pl
from jax.experimental.pallas import tpu as pltpu
from jax.sharding import PartitionSpec as P

LEV = 64
TAPS = 15
LANES = 128
WIDE = 256
STEPS = 2
NEAR = 4
HBM = pl.BlockSpec(memory_space=pltpu.HBM)
VMEM = pl.BlockSpec(memory_space=pltpu.VMEM)
SMEM = pl.BlockSpec(memory_space=pltpu.SMEM)
PARAMS = pltpu.CompilerParams(vmem_limit_bytes=32 * 1024 * 1024)


def circulant_kernel(coef_ref, circ_ref):
    lats, n = coef_ref.shape
    for a in range(lats):
        row = coef_ref[a : a + 1].astype(jnp.float32)
        rolled = pltpu.roll(
            jnp.broadcast_to(row, (LANES, n)), 0, 1, stride=1, stride_axis=0
        )
        first = rolled.T.astype(jnp.bfloat16)
        circ_ref[a, :, :LANES] = first
        circ_ref[a, LANES:, LANES:] = first[: n - LANES]
        circ_ref[a, :LANES, LANES:] = first[n - LANES :]


def circulant(coef):
    lats, n = coef.shape
    return pl.pallas_call(
        circulant_kernel,
        in_specs=[VMEM],
        out_specs=VMEM,
        out_shape=jax.ShapeDtypeStruct((lats, n, WIDE), jnp.bfloat16),
        compiler_params=PARAMS,
        cost_estimate=pl.CostEstimate(
            flops=16 * lats * n * LANES, bytes_accessed=2 * lats * n * WIDE, transcendentals=0
        ),
    )(coef)


def zonal_kernel(circ_ref, x_ref, o_ref):
    parts, lats, count, columns = x_ref.shape
    n = parts * count
    for a in range(lats):
        x = x_ref[:, a].reshape(n, columns)
        first = circ_ref[a]
        circ = jnp.concatenate(
            [first] + [jnp.concatenate([first[n - j :], first[: n - j]]) for j in range(WIDE, n, WIDE)],
            axis=1,
        )
        total = jnp.dot(circ, x, preferred_element_type=jnp.float32)
        o_ref[:, a] = total.astype(jnp.bfloat16).reshape(parts, count, columns)


def zonal(circ, x):
    parts, lats, count, columns = x.shape
    n = parts * count
    return pl.pallas_call(
        zonal_kernel,
        in_specs=[VMEM, VMEM],
        out_specs=VMEM,
        out_shape=jax.ShapeDtypeStruct(x.shape, jnp.bfloat16),
        compiler_params=PARAMS,
        cost_estimate=pl.CostEstimate(
            flops=2 * lats * n * n * columns, bytes_accessed=2 * lats * n * n, transcendentals=0
        ),
    )(circ, x)


def band_kernel(taps_ref, band_ref):
    half = (TAPS - 1) // 2
    upper = lax.broadcasted_iota(jnp.int32, band_ref.shape, 0)
    lower = lax.broadcasted_iota(jnp.int32, band_ref.shape, 1)
    offset = jnp.where(upper // LEV == lower // LEV, upper - lower, TAPS)
    band = jnp.zeros(band_ref.shape, jnp.float32)
    for tap in range(TAPS):
        band = jnp.where(offset == tap - half, taps_ref[tap], band)
    band_ref[...] = band.astype(jnp.bfloat16)


def band_matrix(taps, columns):
    return pl.pallas_call(
        band_kernel,
        in_specs=[SMEM],
        out_specs=VMEM,
        out_shape=jax.ShapeDtypeStruct((columns, columns), jnp.bfloat16),
        compiler_params=PARAMS,
    )(taps)


def vertical_kernel(band_ref, x_ref, o_ref):
    rows, count, columns = o_ref.shape
    x = x_ref[pl.ds(pl.program_id(0) * rows, rows)].reshape(rows * count, columns)
    mixed = jnp.dot(x, band_ref[...], preferred_element_type=jnp.float32)
    o_ref[...] = mixed.astype(jnp.bfloat16).reshape(o_ref.shape)


def vertical(band, x):
    lat_rows, count, columns = x.shape
    rows = lat_rows // STEPS
    return pl.pallas_call(
        vertical_kernel,
        grid=(STEPS,),
        in_specs=[VMEM, VMEM],
        out_specs=pl.BlockSpec((rows, count, columns), lambda i: (i, 0, 0)),
        out_shape=jax.ShapeDtypeStruct(x.shape, jnp.bfloat16),
        compiler_params=PARAMS,
        cost_estimate=pl.CostEstimate(
            flops=2 * x.size * columns, bytes_accessed=4 * x.size, transcendentals=0
        ),
    )(band, x)


def copied(copies):
    for copy in copies:
        copy.start()
    for copy in copies:
        copy.wait()


def first_half_kernel(x_ref, o_ref, sem):
    copied([pltpu.make_async_copy(x_ref.at[pl.ds(0, o_ref.shape[0])], o_ref, sem.at[0])])


def first_half(x):
    lat_rows, count, columns = x.shape
    return pl.pallas_call(
        first_half_kernel,
        in_specs=[HBM],
        out_specs=VMEM,
        out_shape=jax.ShapeDtypeStruct((lat_rows // 2, count, columns), jnp.bfloat16),
        scratch_shapes=[pltpu.SemaphoreType.DMA((1,))],
        compiler_params=pltpu.CompilerParams(vmem_limit_bytes=61 * 1024 * 1024),
    )(x)


def second_half_kernel(first, me_ref, x_ref, *refs):
    outs, sem = refs[:-1], refs[-1]
    half = x_ref.shape[0] // 2
    copies = []
    for i in range(len(outs) * NEAR):
        x = x_ref.at[half + (me_ref[0] ^ (first * NEAR + i))]
        out = outs[i // NEAR].at[i % NEAR]
        copies.append(pltpu.make_async_copy(x, out, sem.at[i]))
    copied(copies)


def second_half(me, x, first, arrays):
    _, count, columns = x.shape
    return pl.pallas_call(
        functools.partial(second_half_kernel, first),
        in_specs=[SMEM, HBM],
        out_specs=[VMEM] * arrays,
        out_shape=[jax.ShapeDtypeStruct((NEAR, count, columns), jnp.bfloat16)] * arrays,
        scratch_shapes=[pltpu.SemaphoreType.DMA((arrays * NEAR,))],
        compiler_params=pltpu.CompilerParams(vmem_limit_bytes=61 * 1024 * 1024),
    )(me, x)


def rotations(first):
    n, wide = first.shape
    turned = [jnp.concatenate([first[n - j :], first[: n - j]]) for j in range(wide, n, wide)]
    return jnp.concatenate([first] + turned, axis=1)


def zonal_first_kernel(circ_ref, x_ref, o_ref):
    parts, count, columns = x_ref.shape
    x = x_ref[...].reshape(parts * count, columns)
    total = jnp.dot(rotations(circ_ref[0]), x, preferred_element_type=jnp.float32)
    o_ref[...] = total.astype(jnp.bfloat16).reshape(o_ref.shape)


def zonal_cost(circ, columns, times=1):
    n = circ.shape[1]
    return pl.CostEstimate(
        flops=int(times * 2 * n * n * columns), bytes_accessed=2 * n * n, transcendentals=0
    )


def zonal_first(circ, x):
    return pl.pallas_call(
        zonal_first_kernel,
        in_specs=[VMEM, VMEM],
        out_specs=VMEM,
        out_shape=jax.ShapeDtypeStruct(x.shape, jnp.bfloat16),
        compiler_params=PARAMS,
        cost_estimate=zonal_cost(circ, x.shape[2]),
    )(circ, x)


def distance_of(core, i, far):
    return i % far * NEAR + i // far * 2 + core


def zonal_second_kernel(me_ref, circ_ref, *refs):
    ins, outs, (x, z) = refs[:2], refs[2:-2], refs[-2:]
    parts, count, columns = x.shape
    for core in range(2):
        for i in range(parts // 2):
            r = distance_of(core, i, len(outs))
            x[me_ref[0] ^ r] = ins[core][i]
    total = jnp.dot(
        rotations(circ_ref[1]),
        x[...].reshape(parts * count, columns),
        preferred_element_type=jnp.float32,
    )
    z[...] = total.astype(jnp.bfloat16).reshape(z.shape)
    for r in range(parts):
        outs[r // NEAR][r % NEAR] = z[me_ref[0] ^ r]


def zonal_second(me, circ, blocks):
    half, count, columns = blocks[0].shape
    arrays = 2 * half // NEAR
    return pl.pallas_call(
        zonal_second_kernel,
        in_specs=[SMEM] + [VMEM] * 3,
        out_specs=[VMEM] * arrays,
        out_shape=[jax.ShapeDtypeStruct((NEAR, count, columns), jnp.bfloat16)] * arrays,
        scratch_shapes=[pltpu.VMEM((2 * half, count, columns), jnp.bfloat16)] * 2,
        compiler_params=PARAMS,
        cost_estimate=zonal_cost(circ, columns, 4),
    )(me, circ, *blocks)


def vertical_first_kernel(band_ref, x_ref, o_ref):
    x = x_ref[...].reshape(-1, x_ref.shape[2])
    mixed = jnp.dot(x, band_ref[...], preferred_element_type=jnp.float32)
    o_ref[...] = mixed.astype(jnp.bfloat16).reshape(o_ref.shape)


def vertical_first(band, x):
    parts, count, columns = x.shape
    rows = parts // STEPS
    return pl.pallas_call(
        vertical_first_kernel,
        grid=(STEPS,),
        in_specs=[VMEM, pl.BlockSpec((rows, count, columns), lambda i: (i, 0, 0))],
        out_specs=pl.BlockSpec((rows, count, columns), lambda i: (i, 0, 0)),
        out_shape=jax.ShapeDtypeStruct((2 * parts, count, columns), jnp.bfloat16),
        compiler_params=PARAMS,
    )(band, x)


def vertical_second_kernel(me_ref, band_ref, *refs):
    ins, (o_ref, mixed, sem) = refs[:2], refs[3:]
    parts, count, columns = mixed.shape
    half = parts // 2
    copies = []
    for core in range(2):
        x = ins[core][...].reshape(half * count, columns)
        out = jnp.dot(x, band_ref[...], preferred_element_type=jnp.float32)
        out = out.astype(jnp.bfloat16).reshape(ins[core].shape)
        mixed[core * half : (core + 1) * half] = out
        for i in range(half):
            lat = parts + (me_ref[0] ^ distance_of(core, i, parts // NEAR))
            block = core * half + i
            copy = pltpu.make_async_copy(mixed.at[block], o_ref.at[lat], sem.at[block])
            copy.start()
            copies.append(copy)
    for copy in copies:
        copy.wait()


def vertical_second(me, band, blocks, result):
    half, count, columns = blocks[0].shape
    return pl.pallas_call(
        vertical_second_kernel,
        in_specs=[SMEM] + [VMEM] * 3 + [HBM],
        out_specs=HBM,
        out_shape=jax.ShapeDtypeStruct((4 * half, count, columns), jnp.bfloat16),
        scratch_shapes=[
            pltpu.VMEM((2 * half, count, columns), jnp.bfloat16),
            pltpu.SemaphoreType.DMA((2 * half,)),
        ],
        input_output_aliases={4: 0},
        compiler_params=PARAMS,
    )(me, band, *blocks, result)


def hop(x, distance, parts):
    return lax.ppermute(x, "lon", [(i, i ^ distance) for i in range(parts)])


def far_hops(arrays, parts):
    return [arrays[0]] + [hop(arrays[i], i * NEAR, parts) for i in range(1, len(arrays))]


def near_hops(arrays, parts):
    far, shape = len(arrays), arrays[0].shape[1:]
    state = jnp.stack(arrays).reshape((far, 2, 2) + shape)
    state = jnp.stack([state[:, 0], hop(state[:, 1], 2, parts)])
    keep, send = (state[:, :, i].reshape((2 * far,) + shape) for i in range(2))
    return keep, hop(send, 1, parts)


def two_ways(fields, zonal_coef, vert_taps, parts):
    lat_rows, count, columns = fields.shape
    position = lax.axis_index("lon")
    me = position.reshape(1)
    swapped = lambda x: lax.all_to_all(x, "lon", 0, 0, tiled=True)
    band = band_matrix(vert_taps.astype(jnp.float32), columns)
    coef = lax.dynamic_index_in_dim(
        zonal_coef.reshape(2, parts, -1), position, 1, keepdims=False
    )
    circ = circulant(coef)
    far = second_half(me, fields, 1, parts // NEAR - 1)
    stays, _ = lax.optimization_barrier((fields, far[0]))
    arrays = far_hops([*second_half(me, stays, 0, 1), *far], parts)
    x = first_half(fields)
    x, _ = lax.optimization_barrier((x, [arrays[1]]))
    mine = swapped(x)
    arrays = near_hops(arrays, parts)
    arrays = zonal_second(me, circ, arrays)
    mine, _ = lax.optimization_barrier((mine, arrays[0]))
    arrays = far_hops(arrays, parts)
    done = zonal_first(circ, mine)
    _, *after = lax.optimization_barrier(((done, band), *arrays))
    done, _ = lax.optimization_barrier((done, [arrays[3]]))
    back = swapped(done)
    blocks = near_hops(after, parts)
    return vertical_second(me, band, blocks, vertical_first(band, back))


def shards(fields, zonal_coef, vert_taps, *, parts):
    lat_rows, count, columns = fields.shape
    lats = lat_rows // parts
    if lats == 2 and parts & (parts - 1) == 0 and parts >= NEAR:
        return two_ways(fields, zonal_coef, vert_taps, parts)
    me = lax.axis_index("lon")
    swapped = lambda x: lax.all_to_all(x, "lon", 0, 0, tiled=True)
    circ = circulant(lax.dynamic_slice_in_dim(zonal_coef, me * lats, lats, 0))
    mine = swapped(fields).reshape(parts, lats, count, columns)
    done = zonal(circ, mine)
    done, taps = lax.optimization_barrier((done, vert_taps.astype(jnp.float32)))
    band = band_matrix(taps, columns)
    return vertical(band, swapped(done.reshape(fields.shape)))


def solution(mesh):
    placed = (P("grp", "lon", None), P(), P())
    return jax.shard_map(
        functools.partial(shards, parts=mesh.shape["lon"]),
        mesh=mesh,
        in_specs=placed,
        out_specs=P("grp", "lon", None),
        check_vma=False,
    )
```

```python
import functools

import jax
import jax.numpy as jnp
from jax import lax
from jax.experimental import pallas as pl
from jax.experimental.pallas import tpu as pltpu
from jax.sharding import PartitionSpec as P

LEV = 64
TAPS = 15
LANES = 128
WIDE = 256
STEPS = 1
NEAR = 4
HBM = pl.BlockSpec(memory_space=pltpu.HBM)
VMEM = pl.BlockSpec(memory_space=pltpu.VMEM)
SMEM = pl.BlockSpec(memory_space=pltpu.SMEM)
PARAMS = pltpu.CompilerParams(vmem_limit_bytes=32 * 1024 * 1024)


def circulant_kernel(coef_ref, circ_ref):
    lats, n = coef_ref.shape
    for a in range(lats):
        row = coef_ref[a : a + 1].astype(jnp.float32)
        rolled = pltpu.roll(
            jnp.broadcast_to(row, (LANES, n)), 0, 1, stride=1, stride_axis=0
        )
        first = rolled.T.astype(jnp.bfloat16)
        circ_ref[a, :, :LANES] = first
        circ_ref[a, LANES:, LANES:] = first[: n - LANES]
        circ_ref[a, :LANES, LANES:] = first[n - LANES :]


def circulant(coef):
    lats, n = coef.shape
    return pl.pallas_call(
        circulant_kernel,
        in_specs=[VMEM],
        out_specs=VMEM,
        out_shape=jax.ShapeDtypeStruct((lats, n, WIDE), jnp.bfloat16),
        compiler_params=PARAMS,
        cost_estimate=pl.CostEstimate(
            flops=16 * lats * n * LANES, bytes_accessed=2 * lats * n * WIDE, transcendentals=0
        ),
    )(coef)


def zonal_kernel(circ_ref, x_ref, o_ref):
    parts, lats, count, columns = x_ref.shape
    n = parts * count
    for a in range(lats):
        x = x_ref[:, a].reshape(n, columns)
        first = circ_ref[a]
        circ = jnp.concatenate(
            [first] + [jnp.concatenate([first[n - j :], first[: n - j]]) for j in range(WIDE, n, WIDE)],
            axis=1,
        )
        total = jnp.dot(circ, x, preferred_element_type=jnp.float32)
        o_ref[:, a] = total.astype(jnp.bfloat16).reshape(parts, count, columns)


def zonal(circ, x):
    parts, lats, count, columns = x.shape
    n = parts * count
    return pl.pallas_call(
        zonal_kernel,
        in_specs=[VMEM, VMEM],
        out_specs=VMEM,
        out_shape=jax.ShapeDtypeStruct(x.shape, jnp.bfloat16),
        compiler_params=PARAMS,
        cost_estimate=pl.CostEstimate(
            flops=2 * lats * n * n * columns, bytes_accessed=2 * lats * n * n, transcendentals=0
        ),
    )(circ, x)


def band_kernel(taps_ref, band_ref):
    half = (TAPS - 1) // 2
    upper = lax.broadcasted_iota(jnp.int32, band_ref.shape, 0)
    lower = lax.broadcasted_iota(jnp.int32, band_ref.shape, 1)
    offset = jnp.where(upper // LEV == lower // LEV, upper - lower, TAPS)
    band = jnp.zeros(band_ref.shape, jnp.float32)
    for tap in range(TAPS):
        band = jnp.where(offset == tap - half, taps_ref[tap], band)
    band_ref[...] = band.astype(jnp.bfloat16)


def band_matrix(taps, columns):
    return pl.pallas_call(
        band_kernel,
        in_specs=[SMEM],
        out_specs=VMEM,
        out_shape=jax.ShapeDtypeStruct((columns, columns), jnp.bfloat16),
        compiler_params=PARAMS,
    )(taps)


def vertical_kernel(band_ref, x_ref, o_ref):
    rows, count, columns = o_ref.shape
    x = x_ref[pl.ds(pl.program_id(0) * rows, rows)].reshape(rows * count, columns)
    mixed = jnp.dot(x, band_ref[...], preferred_element_type=jnp.float32)
    o_ref[...] = mixed.astype(jnp.bfloat16).reshape(o_ref.shape)


def vertical(band, x):
    lat_rows, count, columns = x.shape
    rows = lat_rows // STEPS
    return pl.pallas_call(
        vertical_kernel,
        grid=(STEPS,),
        in_specs=[VMEM, VMEM],
        out_specs=pl.BlockSpec((rows, count, columns), lambda i: (i, 0, 0)),
        out_shape=jax.ShapeDtypeStruct(x.shape, jnp.bfloat16),
        compiler_params=PARAMS,
        cost_estimate=pl.CostEstimate(
            flops=2 * x.size * columns, bytes_accessed=4 * x.size, transcendentals=0
        ),
    )(band, x)


def copied(copies):
    for copy in copies:
        copy.start()
    for copy in copies:
        copy.wait()


def first_half_kernel(x_ref, o_ref, sem):
    copied([pltpu.make_async_copy(x_ref.at[pl.ds(0, o_ref.shape[0])], o_ref, sem.at[0])])


def first_half(x):
    lat_rows, count, columns = x.shape
    return pl.pallas_call(
        first_half_kernel,
        in_specs=[HBM],
        out_specs=VMEM,
        out_shape=jax.ShapeDtypeStruct((lat_rows // 2, count, columns), jnp.bfloat16),
        scratch_shapes=[pltpu.SemaphoreType.DMA((1,))],
        compiler_params=pltpu.CompilerParams(vmem_limit_bytes=61 * 1024 * 1024),
    )(x)


def second_half_kernel(first, me_ref, x_ref, *refs):
    outs, sem = refs[:-1], refs[-1]
    half = x_ref.shape[0] // 2
    copies = []
    for i in range(len(outs) * NEAR):
        x = x_ref.at[half + (me_ref[0] ^ (first * NEAR + i))]
        out = outs[i // NEAR].at[i % NEAR]
        copies.append(pltpu.make_async_copy(x, out, sem.at[i]))
    copied(copies)


def second_half(me, x, first, arrays):
    _, count, columns = x.shape
    return pl.pallas_call(
        functools.partial(second_half_kernel, first),
        in_specs=[SMEM, HBM],
        out_specs=[VMEM] * arrays,
        out_shape=[jax.ShapeDtypeStruct((NEAR, count, columns), jnp.bfloat16)] * arrays,
        scratch_shapes=[pltpu.SemaphoreType.DMA((arrays * NEAR,))],
        compiler_params=pltpu.CompilerParams(vmem_limit_bytes=61 * 1024 * 1024),
    )(me, x)


def rotations(first):
    n, wide = first.shape
    turned = [jnp.concatenate([first[n - j :], first[: n - j]]) for j in range(wide, n, wide)]
    return jnp.concatenate([first] + turned, axis=1)


def zonal_first_kernel(circ_ref, x_ref, o_ref):
    parts, count, columns = x_ref.shape
    x = x_ref[...].reshape(parts * count, columns)
    total = jnp.dot(rotations(circ_ref[0]), x, preferred_element_type=jnp.float32)
    o_ref[...] = total.astype(jnp.bfloat16).reshape(o_ref.shape)


def zonal_cost(circ, columns, times=1):
    n = circ.shape[1]
    return pl.CostEstimate(
        flops=int(times * 2 * n * n * columns), bytes_accessed=2 * n * n, transcendentals=0
    )


def zonal_first(circ, x):
    return pl.pallas_call(
        zonal_first_kernel,
        in_specs=[VMEM, VMEM],
        out_specs=VMEM,
        out_shape=jax.ShapeDtypeStruct(x.shape, jnp.bfloat16),
        compiler_params=PARAMS,
        cost_estimate=zonal_cost(circ, x.shape[2]),
    )(circ, x)


def distance_of(core, i, far):
    return i % far * NEAR + i // far * 2 + core


def zonal_second_kernel(me_ref, circ_ref, *refs):
    ins, outs, (x, z) = refs[:2], refs[2:-2], refs[-2:]
    parts, count, columns = x.shape
    for core in range(2):
        for i in range(parts // 2):
            r = distance_of(core, i, len(outs))
            x[me_ref[0] ^ r] = ins[core][i]
    total = jnp.dot(
        rotations(circ_ref[1]),
        x[...].reshape(parts * count, columns),
        preferred_element_type=jnp.float32,
    )
    z[...] = total.astype(jnp.bfloat16).reshape(z.shape)
    for r in range(parts):
        outs[r // NEAR][r % NEAR] = z[me_ref[0] ^ r]


def zonal_second(me, circ, blocks):
    half, count, columns = blocks[0].shape
    arrays = 2 * half // NEAR
    return pl.pallas_call(
        zonal_second_kernel,
        in_specs=[SMEM] + [VMEM] * 3,
        out_specs=[VMEM] * arrays,
        out_shape=[jax.ShapeDtypeStruct((NEAR, count, columns), jnp.bfloat16)] * arrays,
        scratch_shapes=[pltpu.VMEM((2 * half, count, columns), jnp.bfloat16)] * 2,
        compiler_params=PARAMS,
        cost_estimate=zonal_cost(circ, columns, 4),
    )(me, circ, *blocks)


def vertical_first_kernel(band_ref, x_ref, o_ref):
    x = x_ref[...].reshape(-1, x_ref.shape[2])
    mixed = jnp.dot(x, band_ref[...], preferred_element_type=jnp.float32)
    o_ref[...] = mixed.astype(jnp.bfloat16).reshape(o_ref.shape)


def vertical_first(band, x):
    parts, count, columns = x.shape
    rows = parts // STEPS
    return pl.pallas_call(
        vertical_first_kernel,
        grid=(STEPS,),
        in_specs=[VMEM, pl.BlockSpec((rows, count, columns), lambda i: (i, 0, 0))],
        out_specs=pl.BlockSpec((rows, count, columns), lambda i: (i, 0, 0)),
        out_shape=jax.ShapeDtypeStruct((2 * parts, count, columns), jnp.bfloat16),
        compiler_params=PARAMS,
    )(band, x)


def vertical_second_kernel(me_ref, band_ref, *refs):
    ins, (o_ref, mixed, sem) = refs[:2], refs[3:]
    parts, count, columns = mixed.shape
    half = parts // 2
    copies = []
    for core in range(2):
        x = ins[core][...].reshape(half * count, columns)
        out = jnp.dot(x, band_ref[...], preferred_element_type=jnp.float32)
        out = out.astype(jnp.bfloat16).reshape(ins[core].shape)
        mixed[core * half : (core + 1) * half] = out
        for i in range(half):
            lat = parts + (me_ref[0] ^ distance_of(core, i, parts // NEAR))
            block = core * half + i
            copy = pltpu.make_async_copy(mixed.at[block], o_ref.at[lat], sem.at[block])
            copy.start()
            copies.append(copy)
    for copy in copies:
        copy.wait()


def vertical_second(me, band, blocks, result):
    half, count, columns = blocks[0].shape
    return pl.pallas_call(
        vertical_second_kernel,
        in_specs=[SMEM] + [VMEM] * 3 + [HBM],
        out_specs=HBM,
        out_shape=jax.ShapeDtypeStruct((4 * half, count, columns), jnp.bfloat16),
        scratch_shapes=[
            pltpu.VMEM((2 * half, count, columns), jnp.bfloat16),
            pltpu.SemaphoreType.DMA((2 * half,)),
        ],
        input_output_aliases={4: 0},
        compiler_params=PARAMS,
    )(me, band, *blocks, result)


def hop(x, distance, parts):
    return lax.ppermute(x, "lon", [(i, i ^ distance) for i in range(parts)])


def far_hops(arrays, parts):
    return [arrays[0]] + [hop(arrays[i], i * NEAR, parts) for i in range(1, len(arrays))]


def near_hops(arrays, parts):
    far, shape = len(arrays), arrays[0].shape[1:]
    state = jnp.stack(arrays).reshape((far, 2, 2) + shape)
    state = jnp.stack([state[:, 0], hop(state[:, 1], 2, parts)])
    keep, send = (state[:, :, i].reshape((2 * far,) + shape) for i in range(2))
    return keep, hop(send, 1, parts)


def two_ways(fields, zonal_coef, vert_taps, parts):
    lat_rows, count, columns = fields.shape
    position = lax.axis_index("lon")
    me = position.reshape(1)
    swapped = lambda x: lax.all_to_all(x, "lon", 0, 0, tiled=True)
    band = band_matrix(vert_taps.astype(jnp.float32), columns)
    coef = lax.dynamic_index_in_dim(
        zonal_coef.reshape(2, parts, -1), position, 1, keepdims=False
    )
    circ = circulant(coef)
    far = second_half(me, fields, 1, parts // NEAR - 1)
    stays, _ = lax.optimization_barrier((fields, far[0]))
    arrays = far_hops([*second_half(me, stays, 0, 1), *far], parts)
    x = first_half(fields)
    x, _ = lax.optimization_barrier((x, [arrays[1]]))
    mine = swapped(x)
    arrays = near_hops(arrays, parts)
    arrays = zonal_second(me, circ, arrays)
    mine, _ = lax.optimization_barrier((mine, arrays[0]))
    arrays = far_hops(arrays, parts)
    done = zonal_first(circ, mine)
    _, *after = lax.optimization_barrier(((done, band), *arrays))
    done, _ = lax.optimization_barrier((done, [arrays[3]]))
    back = swapped(done)
    blocks = near_hops(after, parts)
    return vertical_second(me, band, blocks, vertical_first(band, back))


def shards(fields, zonal_coef, vert_taps, *, parts):
    lat_rows, count, columns = fields.shape
    lats = lat_rows // parts
    if lats == 2 and parts & (parts - 1) == 0 and parts >= NEAR:
        return two_ways(fields, zonal_coef, vert_taps, parts)
    me = lax.axis_index("lon")
    swapped = lambda x: lax.all_to_all(x, "lon", 0, 0, tiled=True)
    circ = circulant(lax.dynamic_slice_in_dim(zonal_coef, me * lats, lats, 0))
    mine = swapped(fields).reshape(parts, lats, count, columns)
    done = zonal(circ, mine)
    done, taps = lax.optimization_barrier((done, vert_taps.astype(jnp.float32)))
    band = band_matrix(taps, columns)
    return vertical(band, swapped(done.reshape(fields.shape)))


def solution(mesh):
    placed = (P("grp", "lon", None), P(), P())
    return jax.shard_map(
        functools.partial(shards, parts=mesh.shape["lon"]),
        mesh=mesh,
        in_specs=placed,
        out_specs=P("grp", "lon", None),
        check_vma=False,
    )
```
